256 devices in a mesh: context: 16 (over y_hi, z), tensor: 8 (over x, y_lo), dp: 2 (over core).
Axes of the slice: x: 4, y: 4 (y_hi: 2, y_lo: 2; y = y_hi * 2 + y_lo), z: 8, core: 2. Of those that a mesh axis runs over, the one named last changes fastest.
Arguments:
- turn_q: bfloat16 [16384, 8192], P(('dp', 'context'), 'tensor'), parts along dimension 0, may hold values from -5 to 5
- new_turn_keys: bfloat16 [16384, 1024], P(('dp', 'context'), 'tensor'), parts along dimension 0, may hold values from -5 to 5
- new_turn_values: bfloat16 [16384, 1024], P(('dp', 'context'), 'tensor'), parts along dimension 0, may hold values from -6 to 6
- block_mask: int32 [16, 16], replicated, may hold values from 0 to 1, as said below
- query_dec: bfloat16 [32, 4, 8192], P('dp', None, 'tensor'), parts along dimension 0, may hold values from -5 to 5
- cache_keys: bfloat16 [32, 16384, 1024], P('dp', 'context', 'tensor'), parts along dimension 0, may hold values from -5 to 5
- stream_cache_values: bfloat16 [32, 16384, 1024], P('dp', 'context', 'tensor'), parts along dimension 0, may hold values from -6 to 6
- hist_lengths: int32 [32], P('dp'), parts along dimension 0, may hold values from 1 to 16380, as said below
Outputs:
- turn_out: bfloat16 [16384, 8192], P(('dp', 'context'), 'tensor'), parts along dimension 0
- stream_out: bfloat16 [32, 4, 8192], P(('dp', 'context'), None, 'tensor'), parts along dimension 0
The draws below stay inside these ranges and needn't reach their ends.
There are 2 independent parts, one for each index of `dp`. The reference program is written for one: setup_inputs(seed, part) draws one part's arguments, and reference() takes and returns one part's arrays. A program takes and returns all parts, laid end to end along the dimension named above; an argument that names none is the same for every part. Nothing has to cross between parts.
Inputs may be any that keep to these rules, and one draw needn't show every extreme that they name: `block_mask`: zero above the diagonal; one on the diagonal and in column 0; in each row the ones outside column 0 form a run that ends at the diagonal and spans at most 4 blocks, and in some row it spans exactly 4. `hist_lengths`: at least one stream has the largest value.
All inputs are finite; a program needn't handle non-finite values.
Results may differ from the reference program's by a relative error of at most 0.019.
Values may be sent and summed in bfloat16 or wider, within the bound.
A program may use at most 64 MiB of HBM per device.

```python
import jax
import jax.numpy as jnp
from jax import lax

QUERY_HEADS = 64
KEY_VALUE_HEADS = 8
HEAD_SIZE = 128
TOK_DEV = 512
WIN = 4
STREAM_TOKENS = 4
DECODE_STREAMS = 16
TURN_TOKENS = 8192
TURN_BLOCK_COUNT = 16
CACHE_POSITIONS = 16384


def draw_turn_q(key, part):
    key = jax.random.fold_in(key, 1)
    field_name = jnp.clip(jax.random.normal(key, (TURN_TOKENS, QUERY_HEADS * HEAD_SIZE)), -5.0, 5.0)
    return field_name.astype(jnp.bfloat16)


def draw_new_turn_keys(key, part):
    key = jax.random.fold_in(key, 2)
    field_name = jnp.clip(jax.random.normal(key, (TURN_TOKENS, KEY_VALUE_HEADS * HEAD_SIZE)), -5.0, 5.0)
    return field_name.astype(jnp.bfloat16)


def draw_block_mask(key, part):
    key = jax.random.fold_in(key, 11)
    width_key, row_key = jax.random.split(key)
    widths = jax.random.randint(width_key, (TURN_BLOCK_COUNT,), 1, WIN + 1)
    full_row = jax.random.randint(row_key, (), WIN, TURN_BLOCK_COUNT)
    rows = jnp.arange(TURN_BLOCK_COUNT)
    widths = jnp.where(rows == full_row, WIN, widths)
    row_grid = rows[:, None]
    col_grid = rows[None, :]
    allowed = (col_grid <= row_grid) & ((col_grid == 0) | (row_grid - col_grid < widths[:, None]))
    return allowed.astype(jnp.int32)


def draw_query_dec(key, part):
    key = jax.random.fold_in(key, 3)
    field_name = jnp.clip(jax.random.normal(key, (DECODE_STREAMS, STREAM_TOKENS, QUERY_HEADS * HEAD_SIZE)), -5.0, 5.0)
    return field_name.astype(jnp.bfloat16)


def draw_cache_keys(key, part):
    key = jax.random.fold_in(key, 4)
    field_name = jnp.clip(jax.random.normal(key, (DECODE_STREAMS, CACHE_POSITIONS, KEY_VALUE_HEADS * HEAD_SIZE)), -5.0, 5.0)
    return field_name.astype(jnp.bfloat16)


def draw_hist_lengths(key, part):
    key = jax.random.fold_in(key, 13)
    value_key, chosen_key = jax.random.split(key)
    drawn = jax.random.randint(value_key, (DECODE_STREAMS,), 1, CACHE_POSITIONS - STREAM_TOKENS + 1)
    chosen = jax.random.randint(chosen_key, (), 0, DECODE_STREAMS)
    return jnp.where(jnp.arange(DECODE_STREAMS) == chosen, CACHE_POSITIONS - STREAM_TOKENS, drawn).astype(jnp.int32)


def levels(own_key, extent, pieces, least, largest):
    gain, own = 1.0, jax.random.fold_in(own_key, 6)
    for position, parts in pieces:
        heights = jnp.exp(jax.random.uniform(jax.random.fold_in(own, position), (parts,), jnp.float32, least / len(pieces), largest / len(pieces)))
        gain = gain * jnp.repeat(heights, extent[position] // parts).reshape([-1 if axis == position else 1 for axis in range(len(extent))])
    return gain


def bell_draw(own_key, extent, spread, reach, cuts=(), dtype=jnp.bfloat16):
    values = spread * jax.random.normal(own_key, extent, jnp.float32)
    if cuts:
        values = values * levels(own_key, extent, cuts, -0.22, 0.18)
    return jnp.clip(values, -reach, reach).astype(dtype)


def setup_inputs(seed: int = 0, part: int = 0) -> dict:
    seeds = jax.random.split(jax.random.key(seed), 9)
    part_keys = jax.random.split(jax.random.fold_in(seeds[8], part), 9)
    return {
        "turn_q": draw_turn_q(jax.random.fold_in(jax.random.fold_in(seeds[8], part), 71), part),
        "new_turn_keys": draw_new_turn_keys(jax.random.fold_in(jax.random.fold_in(seeds[8], part), 71), part),
        "new_turn_values": bell_draw(part_keys[2], (TURN_TOKENS, KEY_VALUE_HEADS * HEAD_SIZE), 1.0, 6.0, ((0, 16), (1, 8))),
        "block_mask": draw_block_mask(jax.random.fold_in(seeds[8], 71), part),
        "query_dec": draw_query_dec(jax.random.fold_in(jax.random.fold_in(seeds[8], part), 71), part),
        "cache_keys": draw_cache_keys(jax.random.fold_in(jax.random.fold_in(seeds[8], part), 71), part),
        "stream_cache_values": bell_draw(part_keys[6], (DECODE_STREAMS, CACHE_POSITIONS, KEY_VALUE_HEADS * HEAD_SIZE), 1.0, 6.0, ((1, 16), (2, 8))),
        "hist_lengths": draw_hist_lengths(jax.random.fold_in(jax.random.fold_in(seeds[8], part), 71), part),
    }


MASKED_SCORE = -1e30


def prefill_head(query_head, key_head, value_head, block_mask):
    scale_factor = HEAD_SIZE ** -0.5
    query_blocks = query_head.reshape(TURN_BLOCK_COUNT, TOK_DEV, HEAD_SIZE)
    key_blocks = key_head.reshape(TURN_BLOCK_COUNT, TOK_DEV, HEAD_SIZE)
    value_blocks = value_head.reshape(TURN_BLOCK_COUNT, TOK_DEV, HEAD_SIZE)
    within = jnp.arange(TOK_DEV)[:, None] >= jnp.arange(TOK_DEV)[None, :]

    def query_block(row_block):
        query_matrix = query_blocks[row_block]

        def scores_for(col_block):
            def computed():
                scores = jnp.dot(query_matrix, key_blocks[col_block].T, precision=lax.Precision.HIGHEST) * scale_factor
                return jnp.where((col_block < row_block) | within, scores, MASKED_SCORE)

            def skipped():
                return jnp.full((TOK_DEV, TOK_DEV), MASKED_SCORE, jnp.float32)

            return lax.cond(block_mask[row_block, col_block] > 0, computed, skipped)

        scores = lax.map(scores_for, jnp.arange(TURN_BLOCK_COUNT))
        highest = jnp.max(scores, axis=(0, 2))
        weights = jnp.where(scores > 0.5 * MASKED_SCORE, jnp.exp(scores - highest[None, :, None]), 0.0)
        weight_sum = jnp.sum(weights, axis=(0, 2))
        rounded = lax.optimization_barrier(weights.astype(jnp.bfloat16)).astype(jnp.float32)

        def values_for(col_block):
            def computed():
                return jnp.dot(rounded[col_block], value_blocks[col_block], precision=lax.Precision.HIGHEST)

            def skipped():
                return jnp.zeros((TOK_DEV, HEAD_SIZE), jnp.float32)

            return lax.cond(block_mask[row_block, col_block] > 0, computed, skipped)

        weighted = jnp.sum(lax.map(values_for, jnp.arange(TURN_BLOCK_COUNT)), axis=0)
        return weighted / weight_sum[:, None]

    return lax.map(query_block, jnp.arange(TURN_BLOCK_COUNT))


def stream_head_all(rows_of_queries, rows_of_keys, rows_of_values, length_one):
    query_groups = QUERY_HEADS // KEY_VALUE_HEADS
    query_matrix = rows_of_queries.astype(jnp.float32).reshape(STREAM_TOKENS, KEY_VALUE_HEADS, query_groups, HEAD_SIZE)
    heads_of_keys = rows_of_keys.astype(jnp.float32).reshape(CACHE_POSITIONS, KEY_VALUE_HEADS, HEAD_SIZE)
    heads_of_values = rows_of_values.astype(jnp.float32).reshape(CACHE_POSITIONS, KEY_VALUE_HEADS, HEAD_SIZE)
    scores = jnp.einsum("thgd,phd->hgtp", query_matrix, heads_of_keys, precision=lax.Precision.HIGHEST) * (HEAD_SIZE ** -0.5)
    positions = jnp.arange(CACHE_POSITIONS)
    limit_pos = length_one + 1 + jnp.arange(STREAM_TOKENS)
    usable = positions[None, :] < limit_pos[:, None]
    scores = jnp.where(usable, scores, MASKED_SCORE)
    highest = jnp.max(scores, axis=-1)
    weights = jnp.where(usable, jnp.exp(scores - highest[..., None]), 0.0)
    weight_sum = jnp.sum(weights, axis=-1)
    rounded = lax.optimization_barrier(weights.astype(jnp.bfloat16)).astype(jnp.float32)
    weighted = jnp.einsum("hgtp,phd->hgtd", rounded, heads_of_values, precision=lax.Precision.HIGHEST)
    result = weighted / weight_sum[..., None]
    return result.transpose(2, 0, 1, 3).reshape(STREAM_TOKENS, QUERY_HEADS * HEAD_SIZE).astype(jnp.bfloat16)


def reference(turn_q, new_turn_keys, new_turn_values, block_mask, query_dec, cache_keys, stream_cache_values, hist_lengths):
    query_groups = QUERY_HEADS // KEY_VALUE_HEADS
    query_all = turn_q.astype(jnp.float32).reshape(TURN_TOKENS, QUERY_HEADS, HEAD_SIZE).transpose(1, 0, 2)
    every_key = new_turn_keys.astype(jnp.float32).reshape(TURN_TOKENS, KEY_VALUE_HEADS, HEAD_SIZE).transpose(1, 0, 2)
    every_value = new_turn_values.astype(jnp.float32).reshape(TURN_TOKENS, KEY_VALUE_HEADS, HEAD_SIZE).transpose(1, 0, 2)

    def per_head(head_index):
        group_index = head_index // query_groups
        return prefill_head(query_all[head_index], every_key[group_index], every_value[group_index], block_mask)

    heads_out = lax.map(per_head, jnp.arange(QUERY_HEADS))
    turn_out = heads_out.reshape(QUERY_HEADS, TURN_TOKENS, HEAD_SIZE).transpose(1, 0, 2).reshape(TURN_TOKENS, QUERY_HEADS * HEAD_SIZE).astype(jnp.bfloat16)

    def per_stream(packed):
        return stream_head_all(packed[0], packed[1], packed[2], packed[3])

    stream_out = lax.map(per_stream, (query_dec, cache_keys, stream_cache_values, hist_lengths))
    return turn_out, stream_out
```

```python
import math

import jax
import jax.numpy as jnp
from jax import lax
from jax.experimental import pallas as pl
from jax.experimental.pallas import tpu as pltpu
from jax.sharding import PartitionSpec as P

HEAD = 128
HEADS = 8
BLOCK = 512
STREAMS = 16
TOKENS = 4
ROWS = HEADS * TOKENS
CTX = 16
RING = 8
VROWS = 144
PACK = 48
SCALE = HEAD**-0.5 * math.log2(math.e)
NEG = -1e30
F32, BF16 = jnp.float32, jnp.bfloat16
NT = (((1,), (1,)), ((), ()))
MESH = pl.DeviceIdType.MESH


def kernel(
    mask_ref, hist_ref, k_ref, v_ref, qd_ref, q_hbm, ck_hbm, cv_hbm,
    out_ref, sout_ref,
    qv, qt, kb, vt, acc, m_ref, s0, s1, x0, x1,
    ck, cv, d0, d1, e0, e1, part, got,
    local_sem, ss, rs, pss, prs,
):
    c = lax.axis_index("context")
    shard = ck_hbm.shape[1]

    q_copy = pltpu.make_async_copy(q_hbm, qv, local_sem.at[2, 0])
    q_copy.start()
    caches = []
    for s in range(STREAMS):
        pair = (
            pltpu.make_async_copy(ck_hbm.at[s], ck.at[s], local_sem.at[0, s]),
            pltpu.make_async_copy(cv_hbm.at[s], cv.at[s], local_sem.at[1, s]),
        )
        caches.append(pair)

    barrier = pltpu.get_barrier_semaphore()
    for k in range(1, CTX):
        pl.semaphore_signal(
            barrier, inc=1, device_id={"context": lax.rem(c + k, CTX)}, device_id_type=MESH
        )
    vt[0, :HEAD, :] = v_ref[...].T
    vt[:, HEAD:, :] = jnp.ones((5, VROWS - HEAD, BLOCK), BF16)
    pl.semaphore_wait(barrier, CTX - 1)

    def k_at(slot):
        return k_ref if slot == 0 else kb.at[slot]

    def v_at(slot):
        return vt.at[slot, pl.ds(0, HEAD)]

    def send(what, slot, to, to_slot, sem):
        copy = pltpu.make_async_remote_copy(
            src_ref=k_at(slot) if what == 0 else v_at(slot),
            dst_ref=kb.at[to_slot] if what == 0 else v_at(to_slot),
            send_sem=ss.at[sem],
            recv_sem=rs.at[2 * to_slot + what],
            device_id={"context": to},
            device_id_type=MESH,
        )
        return copy

    def arrived(what, slot):
        send(what, slot, c, slot, 0).wait_recv()

    def first_block(stage):
        def at(index, stage_of, copies):
            if stage_of == stage:
                yield index, copies

        yield from at(0, 0, [(0, 0, 3, 3, 6), (1, 0, 3, 3, 7), (0, 0, 7, 4, 10), (0, 0, 6, 4, 11), (1, 0, 15, 4, 12), (1, 0, 14, 4, 13), (0, 0, 8, 4, 8), (1, 0, 8, 4, 9)])
        yield from at(1, 1, [(0, 1, 9, 4, 6), (1, 1, 9, 4, 7)])
        yield from at(6, 1, [(0, 4, 4, 4, 6), (0, 4, 5, 4, 7), (0, 4, 14, 4, 8)])
        yield from at(14, 1, [(1, 4, 12, 4, 6), (1, 4, 13, 4, 7), (1, 4, 6, 4, 8)])
        yield from at(7, 1, [(0, 4, 15, 4, 6)])
        yield from at(15, 1, [(1, 4, 7, 4, 6)])
        yield from at(2, 2, [(0, 2, 10, 4, 6), (1, 2, 10, 4, 7)])
        yield from at(3, 2, [(0, 3, 11, 4, 6), (1, 3, 11, 4, 7)])
        yield from at(5, 2, [(0, 4, 13, 4, 6)])
        yield from at(13, 2, [(1, 4, 5, 4, 6)])
        yield from at(4, 2, [(0, 4, 12, 4, 6)])
        yield from at(12, 2, [(1, 4, 4, 4, 6)])

    def start_first(stage):
        for index, copies in first_block(stage):

            @pl.when(c == index)
            def _(copies=copies):
                waited = set()
                for what, slot, to, to_slot, sem in copies:
                    if slot >= 3 and (what, slot) not in waited:
                        waited.add((what, slot))
                        arrived(what, slot)
                    send(what, slot, to, to_slot, sem).start()

    def wait_first():
        for stage in range(3):
            for index, copies in first_block(stage):

                @pl.when(c == index)
                def _(copies=copies):
                    for what, slot, to, to_slot, sem in copies:
                        send(what, slot, to, to_slot, sem).wait_send()

    nxt = jnp.minimum(c + 1, CTX - 1)

    def forward(slot, lowest, waits):
        for what in range(2):
            if waits:

                @pl.when(c >= slot)
                def _():
                    arrived(what, slot)

            if slot < 3:

                @pl.when((c >= lowest) & (c < CTX - 1))
                def _():
                    send(what, slot, nxt, slot + 1, 2 * slot + what).start()

    forward(0, 0, False)
    start_first(0)

    for k_copy, v_copy in caches:
        k_copy.start()
        v_copy.start()
    q_copy.wait()
    for h in range(HEADS):
        head = qv[:, h * HEAD : (h + 1) * HEAD].astype(F32) * SCALE
        qt[h] = head.astype(BF16).T

    sb, xb = (s0, s1), (x0, x1)

    def scores(slot, h, diagonal):
        s = jnp.dot(k_at(slot)[...], qt[h], preferred_element_type=F32)
        if diagonal:
            key = lax.broadcasted_iota(jnp.int32, s.shape, 0)
            query = lax.broadcasted_iota(jnp.int32, s.shape, 1)
            s = jnp.where(key <= query, s, NEG)
        sb[h % 2][...] = s
        xb[h % 2][...] = jnp.max(s, axis=0, keepdims=True)

    def weigh(slot, h, bias):
        top = xb[h % 2][...]
        if bias is None:
            new = shift = top
        else:
            old = m_ref[h, :1, :]
            new = jnp.maximum(old, top + bias)
            shift = new - bias
        p = jnp.exp2(sb[h % 2][...] - shift).astype(BF16)
        pv = jnp.dot(vt[slot], p, preferred_element_type=F32)
        if bias is None:
            acc[h] = pv
        else:
            acc[h] = acc[h] * jnp.exp2(old - new) + pv
        m_ref[h, :1, :] = new

    def attend(slot, bias, diagonal=False):
        scores(slot, 0, diagonal)
        for h in range(HEADS):
            if h + 1 < HEADS:
                scores(slot, h + 1, diagonal)
            weigh(slot, h, bias)

    def attend_slot(slot):
        column = jnp.maximum(c - slot, 0) if slot < 4 else 0
        bias = jnp.where(mask_ref[c, column] > 0, 0.0, NEG)

        @pl.when(c >= slot)
        def _():
            attend(slot, bias)

    attend(0, None, True)

    db, eb = (d0, d1), (e0, e1)
    col = lax.broadcasted_iota(jnp.int32, (ROWS, shard), 1)
    token = lax.rem(lax.broadcasted_iota(jnp.int32, (ROWS, shard), 0), TOKENS)
    ahead = col - token
    eye = lax.broadcasted_iota(jnp.int32, (ROWS, HEAD), 0) == lax.broadcasted_iota(
        jnp.int32, (ROWS, HEAD), 1
    )
    line = lax.broadcasted_iota(jnp.int32, (PACK - ROWS, HEAD), 0)

    def stream_scores(s, b):
        pltpu.make_async_copy(ck_hbm.at[s], ck.at[s], local_sem.at[0, s]).wait()
        rows = qd_ref[s].astype(F32) * SCALE
        rows = jnp.concatenate(
            [rows[:, g * HEAD : (g + 1) * HEAD] for g in range(HEADS)], axis=0
        ).astype(BF16)
        x = lax.dot_general(rows, ck[s], NT, preferred_element_type=F32)
        limit = hist_ref[s] + 1 - c * shard
        x = jnp.where(ahead < limit, x, NEG)
        db[b][...] = x
        eb[b][...] = jnp.broadcast_to(jnp.max(x, axis=1, keepdims=True), (ROWS, HEAD))

    def stream_weigh(s, b):
        pltpu.make_async_copy(cv_hbm.at[s], cv.at[s], local_sem.at[1, s]).wait()
        top = eb[b][:, :1]
        p = jnp.exp2(db[b][...] - top)
        total = jnp.sum(p, axis=1, keepdims=True)
        o = jnp.dot(p.astype(BF16), cv[s], preferred_element_type=F32) / total
        part[s, :ROWS, :] = o.astype(BF16)
        level = top + jnp.log(total) * math.log2(math.e)
        level = jnp.sum(jnp.where(eye, level, 0.0), axis=0, keepdims=True)
        high = level.astype(BF16).astype(F32)
        mid = (level - high).astype(BF16).astype(F32)
        low = level - high - mid
        packed = jnp.where(line == 0, high, jnp.where(line == 1, mid, jnp.where(line == 2, low, 0.0)))
        part[s, ROWS:, :] = packed.astype(BF16)

    stream_scores(0, 0)

    def streams(i, carry):
        for u in range(4):
            s = i * 4 + u
            stream_scores(s + 1, (u + 1) % 2)
            stream_weigh(s, u % 2)
        return carry

    lax.fori_loop(0, STREAMS // 4 - 1, streams, 0)
    for s in range(STREAMS - 4, STREAMS):
        if s + 1 < STREAMS:
            stream_scores(s + 1, (s + 1) % 2)
        stream_weigh(s, s % 2)

    forward(1, 1, True)
    start_first(1)

    def partial(k):
        to = lax.rem(c + k, CTX)
        return pltpu.make_async_remote_copy(
            src_ref=part.at[to],
            dst_ref=got.at[c],
            send_sem=pss.at[k],
            recv_sem=prs.at[k],
            device_id={"context": to},
            device_id_type=MESH,
        )

    for k in range(1, CTX):
        partial(k).start()
    got[c] = part[c]

    attend_slot(1)
    forward(2, 3, True)
    start_first(2)
    attend_slot(2)

    for what in range(2):
        kept = (c == 4) | (c == 5) | (c == 6) | (c == 7) | (c >= 8)
        taken = (
            (c == 6) | (c == 7) | (c == 4) | (c == 5)
            if what == 0
            else (c == 14) | (c == 15) | (c == 12) | (c == 13)
        )

        @pl.when(kept & jnp.logical_not(taken))
        def _():
            arrived(what, 4)

    attend_slot(4)

    for what in range(2):

        @pl.when((c >= 3) & (c != 3))
        def _():
            arrived(what, 3)

    attend_slot(3)

    for h in range(HEADS):
        o = acc[h, :HEAD, :] / acc[h, HEAD : HEAD + 1, :]
        out_ref[:, h * HEAD : (h + 1) * HEAD] = o.astype(BF16).T

    for k in range(1, CTX):
        partial(k).wait()

    def level_of(source):
        rows = got[source, ROWS:, :].astype(F32)
        row = rows[0:1, :] + rows[1:2, :] + rows[2:3, :]
        return jnp.sum(jnp.where(eye, row, 0.0), axis=1, keepdims=True)

    levels = [level_of(source) for source in range(CTX)]
    top = levels[0]
    for level in levels[1:]:
        top = jnp.maximum(top, level)
    total = jnp.zeros((ROWS, 1), F32)
    value = jnp.zeros((ROWS, HEAD), F32)
    for source, level in enumerate(levels):
        w = jnp.exp2(level - top)
        total += w
        value += got[source, :ROWS, :].astype(F32) * w
    value = value / total
    for g in range(HEADS):
        sout_ref[0, :, g * HEAD : (g + 1) * HEAD] = value[g * TOKENS : (g + 1) * TOKENS, :].astype(BF16)

    for slot in range(3):
        lowest = (0, 1, 3)[slot]
        for what in range(2):

            @pl.when((c >= lowest) & (c < CTX - 1))
            def _():
                send(what, slot, nxt, slot + 1, 2 * slot + what).wait_send()

    wait_first()


def local(turn_q, keys, values, block_mask, query_dec, cache_keys, cache_values, lengths):
    vmem = pl.BlockSpec(memory_space=pltpu.VMEM)
    smem = pl.BlockSpec(memory_space=pltpu.SMEM)
    anywhere = pl.BlockSpec(memory_space=pl.ANY)
    streams, shard, _ = cache_keys.shape
    return pl.pallas_call(
        kernel,
        out_shape=(
            jax.ShapeDtypeStruct(turn_q.shape, BF16),
            jax.ShapeDtypeStruct((1, TOKENS, HEADS * HEAD), BF16),
        ),
        in_specs=[smem, smem, vmem, vmem, vmem, anywhere, anywhere, anywhere],
        out_specs=(vmem, vmem),
        scratch_shapes=[
            pltpu.VMEM((BLOCK, HEADS * HEAD), BF16),
            pltpu.VMEM((HEADS, HEAD, BLOCK), BF16),
            pltpu.VMEM((5, BLOCK, HEAD), BF16),
            pltpu.VMEM((5, VROWS, BLOCK), BF16),
            pltpu.VMEM((HEADS, VROWS, BLOCK), F32),
            pltpu.VMEM((HEADS, 8, BLOCK), F32),
            pltpu.VMEM((BLOCK, BLOCK), F32),
            pltpu.VMEM((BLOCK, BLOCK), F32),
            pltpu.VMEM((1, BLOCK), F32),
            pltpu.VMEM((1, BLOCK), F32),
            pltpu.VMEM((streams, shard, HEAD), BF16),
            pltpu.VMEM((streams, shard, HEAD), BF16),
            pltpu.VMEM((ROWS, shard), F32),
            pltpu.VMEM((ROWS, shard), F32),
            pltpu.VMEM((ROWS, HEAD), F32),
            pltpu.VMEM((ROWS, HEAD), F32),
            pltpu.VMEM((streams, PACK, HEAD), BF16),
            pltpu.VMEM((CTX, PACK, HEAD), BF16),
            pltpu.SemaphoreType.DMA((3, STREAMS)),
            pltpu.SemaphoreType.DMA((14,)),
            pltpu.SemaphoreType.DMA((10,)),
            pltpu.SemaphoreType.DMA((CTX,)),
            pltpu.SemaphoreType.DMA((CTX,)),
        ],
        compiler_params=pltpu.CompilerParams(
            collective_id=0, has_side_effects=True, vmem_limit_bytes=56 * 2**20
        ),
        cost_estimate=pl.CostEstimate(
            flops=6 * 10**9, bytes_accessed=11 * 2**20, transcendentals=11 * 10**6
        ),
    )(block_mask, lengths, keys, values, query_dec, turn_q, cache_keys, cache_values)


def solution(mesh):
    in_specs = (
        P(("dp", "context"), "tensor"),
        P(("dp", "context"), "tensor"),
        P(("dp", "context"), "tensor"),
        P(),
        P("dp", None, "tensor"),
        P("dp", "context", "tensor"),
        P("dp", "context", "tensor"),
        P("dp"),
    )
    out_specs = (P(("dp", "context"), "tensor"), P(("dp", "context"), None, "tensor"))
    return jax.shard_map(local, mesh=mesh, in_specs=in_specs, out_specs=out_specs, check_vma=False)
```

```python
import math

import jax
import jax.numpy as jnp
from jax import lax
from jax.experimental import pallas as pl
from jax.experimental.pallas import tpu as pltpu
from jax.sharding import PartitionSpec as P

HEAD = 128
HEADS = 8
BLOCK = 512
STREAMS = 16
TOKENS = 4
ROWS = HEADS * TOKENS
CTX = 16
RING = 8
VROWS = 144
PACK = 48
GROUP = 4
LOG2E = math.log2(math.e)
SCALE = HEAD**-0.5 * LOG2E
NEG = -1e30
F32, BF16 = jnp.float32, jnp.bfloat16
NT = (((1,), (1,)), ((), ()))
MESH = pl.DeviceIdType.MESH


def kernel(
    mask_ref, hist_ref, k_ref, v_ref, qd_ref, q_hbm, ck_hbm, cv_hbm,
    out_ref, sout_ref,
    qv, qt, vown, km, vm, k0, v0, acc, m_ref, s0, s1, x0, x1,
    ck, cv, d0, d1, e0, e1, tops, totals, part, pair, got,
    local_sem, ss, rs, pss, prs,
):
    c = lax.axis_index("context")
    z = lax.rem(c, RING)
    half = c - z
    other = RING - half
    shard = ck_hbm.shape[1]

    q_copy = pltpu.make_async_copy(q_hbm, qv, local_sem.at[2, 0])
    q_copy.start()
    groups = STREAMS // GROUP

    def cache_copy(which, g):
        here, there = ((ck_hbm, ck), (cv_hbm, cv))[which]
        some = pl.ds(g * GROUP, GROUP)
        return pltpu.make_async_copy(here.at[some], there.at[some], local_sem.at[which, g])

    for ref in (vown, vm, v0):
        index = (Ellipsis, pl.ds(HEAD, VROWS - HEAD), slice(None))
        ref[index] = jnp.ones(ref.shape[:-2] + (VROWS - HEAD, ref.shape[-1]), BF16)

    barrier = pltpu.get_barrier_semaphore()
    for k in range(1, CTX):
        pl.semaphore_signal(
            barrier, inc=1, device_id={"context": lax.rem(c + k, CTX)}, device_id_type=MESH
        )
    vown[:HEAD, :] = v_ref[...].T
    pl.semaphore_wait(barrier, CTX - 1)

    own = (k_ref, vown.at[pl.ds(0, HEAD)])

    def main(what, slot):
        return (km.at[slot - 1], vm.at[slot - 1, pl.ds(0, HEAD)])[what], 2 * (slot - 1) + what

    def zero(what):
        return (k0, v0.at[pl.ds(0, HEAD)])[what], 6 + what

    def copy(source, target, to, sem):
        return pltpu.make_async_remote_copy(
            src_ref=source,
            dst_ref=target[0],
            send_sem=ss.at[sem],
            recv_sem=rs.at[target[1]],
            device_id={"context": to},
            device_id_type=MESH,
        )

    def arrived(target):
        copy(target[0], target, c, 0).wait_recv()

    sent = []

    def start(when, copies):
        @pl.when(when)
        def _():
            for one in copies:
                copy(*one).start()

        sent.append((when, copies))

    def both(make):
        return [make(what) for what in range(2)]

    def await_when(when, targets):
        @pl.when(when)
        def _():
            for target in targets:
                arrived(target)

    nxt = jnp.minimum(c + 1, CTX - 1)

    start(c == 0, both(lambda w: (own[w], zero(w), 6, 6 + w)))
    start(c <= 14, both(lambda w: (own[w], main(w, 1), nxt, w)))
    start(c == 0, both(lambda w: (own[w], main(w, 3), 3, 8 + w)))
    start(c == 0, both(lambda w: (own[w], zero(w), 7, 10 + w)))

    def pass_on(when, slot):
        for w in range(2):
            await_when(c >= slot, [main(w, slot)])
            start(when, [(main(w, slot)[0], main(w, slot + 1), nxt, 2 * slot + w)])

    def first_to(when, what, targets):
        await_when(when, [zero(what)])
        start(when, [(zero(what)[0], zero(what), to, sem) for to, sem in targets])

    def first_both(when, to):
        for w in range(2):
            first_to(when, w, [(to, 6 + w)])

    def across(slot, to):
        start(c == slot, both(lambda w: (main(w, slot)[0], zero(w), to, 6 + w)))

    def stage_two():
        pass_on((c >= 1) & (c <= 14), 1)
        across(1, 9)
        first_to(c == 6, 0, [(4, 6)])

    def stage_three():
        first_to(c == 6, 1, [(4, 7)])
        start(c == 6, both(lambda w: (zero(w)[0], zero(w), 5, 8 + w)))
        start(c == 6, both(lambda w: (zero(w)[0], zero(w), 14, 10 + w)))

    def stage_four():
        pass_on((c >= 3) & (c <= 14), 2)
        across(2, 10)
        first_both(c == 9, 8)
        first_both(c == 7, 15)
        first_both(c == 4, 12)
        await_when(c == 3, both(lambda w: main(w, 3)))
        across(3, 11)

    def stage_five():
        first_both(c == 5, 13)

    for g in range(groups):
        cache_copy(0, g).start()
        cache_copy(1, g).start()
    q_copy.wait()

    sb, xb = (s0, s1), (x0, x1)

    def turn_head(h):
        head = qv[:, h * HEAD : (h + 1) * HEAD].astype(F32) * SCALE
        qt[h] = head.astype(BF16).T

    def scores(keys, h, diagonal):
        s = jnp.dot(keys[...], qt[h], preferred_element_type=F32)
        if diagonal:
            key = lax.broadcasted_iota(jnp.int32, s.shape, 0)
            query = lax.broadcasted_iota(jnp.int32, s.shape, 1)
            s = jnp.where(key <= query, s, NEG)
        sb[h % 2][...] = s
        xb[h % 2][...] = jnp.max(s, axis=0, keepdims=True)

    def weigh(values, bias, h):
        top = xb[h % 2][...]
        if bias is None:
            new = shift = top
        else:
            old = m_ref[h, :1, :]
            new = jnp.maximum(old, top + bias)
            shift = new - bias
        p = jnp.exp2(sb[h % 2][...] - shift).astype(BF16)
        pv = jnp.dot(values[...], p, preferred_element_type=F32)
        if bias is None:
            acc[h] = pv
        else:
            acc[h] = acc[h] * jnp.exp2(old - new) + pv
        m_ref[h, :1, :] = new

    def finish(h):
        o = acc[h, :HEAD, :] / acc[h, HEAD : HEAD + 1, :]
        out_ref[:, h * HEAD : (h + 1) * HEAD] = o.astype(BF16).T

    def attend(keys, values, bias, diagonal=False, last=False):
        if diagonal:
            turn_head(0)
        scores(keys, 0, diagonal)
        for h in range(HEADS):
            if h + 1 < HEADS:
                if diagonal:
                    turn_head(h + 1)
                scores(keys, h + 1, diagonal)
            weigh(values, bias, h)
            if last and h:
                finish(h - 1)
        if last:
            finish(HEADS - 1)

    def attend_main(slot, when, last=False):
        allowed = mask_ref[c, jnp.maximum(c - slot, 0)] > 0
        bias = jnp.where(allowed, 0.0, NEG)

        @pl.when(when)
        def _():
            attend(km.at[slot - 1], vm.at[slot - 1], bias, last=last)

    def attend_zero(when, last=False):
        bias = jnp.where(mask_ref[c, 0] > 0, 0.0, NEG)

        @pl.when(when)
        def _():
            attend(k0, v0, bias, last=last)

    db, eb = (d0, d1), (e0, e1)
    col = lax.broadcasted_iota(jnp.int32, (ROWS, shard), 1)
    token = lax.rem(lax.broadcasted_iota(jnp.int32, (ROWS, shard), 0), TOKENS)
    ahead = col - token
    eye = lax.broadcasted_iota(jnp.int32, (ROWS, HEAD), 0) == lax.broadcasted_iota(
        jnp.int32, (ROWS, HEAD), 1
    )
    line = lax.broadcasted_iota(jnp.int32, (PACK - ROWS, HEAD), 0)

    def stream_scores(s, b):
        rows = qd_ref[s].astype(F32) * SCALE
        rows = jnp.concatenate(
            [rows[:, g * HEAD : (g + 1) * HEAD] for g in range(HEADS)], axis=0
        ).astype(BF16)
        x = lax.dot_general(rows, ck[s], NT, preferred_element_type=F32)
        limit = hist_ref[s] + 1 - c * shard
        x = jnp.where(ahead < limit, x, NEG)
        db[b][...] = x
        eb[b][...] = jnp.broadcast_to(jnp.max(x, axis=1, keepdims=True), (ROWS, HEAD))

    def stream_weigh(s, b):
        top = eb[b][:, :1]
        p = jnp.exp2(db[b][...] - top)
        total = jnp.sum(p, axis=1, keepdims=True)
        o = jnp.dot(p.astype(BF16), cv[s], preferred_element_type=F32) / total
        part[s, :ROWS, :] = o.astype(BF16)
        tops[s] = eb[b][...]
        totals[s] = jnp.broadcast_to(total, (ROWS, HEAD))

    def store_level(ref, s, level):
        level = jnp.sum(jnp.where(eye, level, 0.0), axis=0, keepdims=True)
        high = level.astype(BF16).astype(F32)
        mid = (level - high).astype(BF16).astype(F32)
        low = level - high - mid
        packed = jnp.where(line == 0, high, jnp.where(line == 1, mid, jnp.where(line == 2, low, 0.0)))
        ref[s, ROWS:, :] = packed.astype(BF16)

    def level_of(ref, s):
        rows = ref[s, ROWS:, :].astype(F32)
        row = rows[0:1, :] + rows[1:2, :] + rows[2:3, :]
        return jnp.sum(jnp.where(eye, row, 0.0), axis=1, keepdims=True)

    def streams(first, groups_now):
        stream_scores(first, 0)

        def group(i, carry):
            for u in range(GROUP):
                s = first + i * GROUP + u
                if u + 1 < GROUP:
                    stream_scores(s + 1, (u + 1) % 2)
                else:
                    stream_scores(jnp.minimum(s + 1, STREAMS - 1), (u + 1) % 2)
                stream_weigh(s, u % 2)
            return carry

        lax.fori_loop(0, groups_now, group, 0)

    def cross_copy():
        return pltpu.make_async_remote_copy(
            src_ref=part.at[pl.ds(other, RING)],
            dst_ref=pair,
            send_sem=pss.at[0],
            recv_sem=prs.at[0],
            device_id={"context": lax.rem(c + RING, CTX)},
            device_id_type=MESH,
        )

    def merge_pairs():
        cross_copy().wait()
        for n in range(RING):
            s = half + n
            one, two = level_of(part, s), level_of(pair, n)
            top = jnp.maximum(one, two)
            w_one, w_two = jnp.exp2(one - top), jnp.exp2(two - top)
            total = w_one + w_two
            value = part[s, :ROWS, :].astype(F32) * w_one + pair[n, :ROWS, :].astype(F32) * w_two
            part[s, :ROWS, :] = (value / total).astype(BF16)
            store_level(part, s, top + jnp.log(total) * LOG2E)

    def ring_copy(k):
        to = half + lax.rem(z + k, RING)
        return pltpu.make_async_remote_copy(
            src_ref=part.at[to],
            dst_ref=got.at[z],
            send_sem=pss.at[k],
            recv_sem=prs.at[k],
            device_id={"context": to},
            device_id_type=MESH,
        )

    attend(k_ref, vown, None, True)
    for g in range(groups):
        cache_copy(0, g).wait()
        cache_copy(1, g).wait()
    streams(0, groups // 2)
    stage_two()
    streams(STREAMS // 2, groups // 2)
    stage_three()
    for s in range(STREAMS):
        store_level(part, s, tops[s] + jnp.log(totals[s]) * LOG2E)
    cross_copy().start()
    attend_main(1, c >= 1)
    stage_four()
    attend_main(2, c >= 2)
    stage_five()
    merge_pairs()
    for k in range(1, RING):
        ring_copy(k).start()
    got[z] = part[c]

    sooner = (c == 4) | (c == 6) | (c == 7) | (c == 9) | (c == 14)
    later = (c >= 4) & jnp.logical_not(sooner)
    await_when(c == 14, both(zero))
    attend_zero(sooner)
    await_when(c >= 4, both(lambda w: main(w, 3)))
    attend_main(3, sooner | (c == 3), True)
    attend_main(3, later)
    await_when(later & (c != 5), both(zero))
    attend_zero(later, True)

    @pl.when(c < 3)
    def _():
        for h in range(HEADS):
            finish(h)

    for k in range(1, RING):
        ring_copy(k).wait()
    levels = [level_of(got, n) for n in range(RING)]
    top = levels[0]
    for level in levels[1:]:
        top = jnp.maximum(top, level)
    total = jnp.zeros((ROWS, 1), F32)
    value = jnp.zeros((ROWS, HEAD), F32)
    for n, level in enumerate(levels):
        w = jnp.exp2(level - top)
        total += w
        value += got[n, :ROWS, :].astype(F32) * w
    value = value / total
    for g in range(HEADS):
        sout_ref[0, :, g * HEAD : (g + 1) * HEAD] = value[g * TOKENS : (g + 1) * TOKENS, :].astype(BF16)

    for when, some in sent:

        @pl.when(when)
        def _(some=some):
            for one in some:
                copy(*one).wait_send()


def local(turn_q, keys, values, block_mask, query_dec, cache_keys, cache_values, lengths):
    vmem = pl.BlockSpec(memory_space=pltpu.VMEM)
    smem = pl.BlockSpec(memory_space=pltpu.SMEM)
    anywhere = pl.BlockSpec(memory_space=pl.ANY)
    streams, shard, _ = cache_keys.shape
    return pl.pallas_call(
        kernel,
        out_shape=(
            jax.ShapeDtypeStruct(turn_q.shape, BF16),
            jax.ShapeDtypeStruct((1, TOKENS, HEADS * HEAD), BF16),
        ),
        in_specs=[smem, smem, vmem, vmem, vmem, anywhere, anywhere, anywhere],
        out_specs=(vmem, vmem),
        scratch_shapes=[
            pltpu.VMEM((BLOCK, HEADS * HEAD), BF16),
            pltpu.VMEM((HEADS, HEAD, BLOCK), BF16),
            pltpu.VMEM((VROWS, BLOCK), BF16),
            pltpu.VMEM((3, BLOCK, HEAD), BF16),
            pltpu.VMEM((3, VROWS, BLOCK), BF16),
            pltpu.VMEM((BLOCK, HEAD), BF16),
            pltpu.VMEM((VROWS, BLOCK), BF16),
            pltpu.VMEM((HEADS, VROWS, BLOCK), F32),
            pltpu.VMEM((HEADS, 8, BLOCK), F32),
            pltpu.VMEM((BLOCK, BLOCK), F32),
            pltpu.VMEM((BLOCK, BLOCK), F32),
            pltpu.VMEM((1, BLOCK), F32),
            pltpu.VMEM((1, BLOCK), F32),
            pltpu.VMEM((streams, shard, HEAD), BF16),
            pltpu.VMEM((streams, shard, HEAD), BF16),
            pltpu.VMEM((ROWS, shard), F32),
            pltpu.VMEM((ROWS, shard), F32),
            pltpu.VMEM((ROWS, HEAD), F32),
            pltpu.VMEM((ROWS, HEAD), F32),
            pltpu.VMEM((streams, ROWS, HEAD), F32),
            pltpu.VMEM((streams, ROWS, HEAD), F32),
            pltpu.VMEM((streams, PACK, HEAD), BF16),
            pltpu.VMEM((RING, PACK, HEAD), BF16),
            pltpu.VMEM((RING, PACK, HEAD), BF16),
            pltpu.SemaphoreType.DMA((3, STREAMS // GROUP)),
            pltpu.SemaphoreType.DMA((12,)),
            pltpu.SemaphoreType.DMA((8,)),
            pltpu.SemaphoreType.DMA((RING,)),
            pltpu.SemaphoreType.DMA((RING,)),
        ],
        compiler_params=pltpu.CompilerParams(
            collective_id=0, has_side_effects=True, vmem_limit_bytes=56 * 2**20
        ),
        cost_estimate=pl.CostEstimate(
            flops=6 * 10**9, bytes_accessed=11 * 2**20, transcendentals=11 * 10**6
        ),
    )(block_mask, lengths, keys, values, query_dec, turn_q, cache_keys, cache_values)


def solution(mesh):
    in_specs = (
        P(("dp", "context"), "tensor"),
        P(("dp", "context"), "tensor"),
        P(("dp", "context"), "tensor"),
        P(),
        P("dp", None, "tensor"),
        P("dp", "context", "tensor"),
        P("dp", "context", "tensor"),
        P("dp"),
    )
    out_specs = (P(("dp", "context"), "tensor"), P(("dp", "context"), None, "tensor"))
    return jax.shard_map(local, mesh=mesh, in_specs=in_specs, out_specs=out_specs, check_vma=False)
```

```python
import math

import jax
import jax.numpy as jnp
from jax import lax
from jax.experimental import pallas as pl
from jax.experimental.pallas import tpu as pltpu
from jax.sharding import PartitionSpec as P

HEAD = 128
HEADS = 8
BLOCK = 512
STREAMS = 16
TOKENS = 4
ROWS = HEADS * TOKENS
CTX = 16
RING = 8
VROWS = 144
PACK = 48
GROUP = 4
LOG2E = math.log2(math.e)
SCALE = HEAD**-0.5 * LOG2E
NEG = -1e30
F32, BF16 = jnp.float32, jnp.bfloat16
NT = (((1,), (1,)), ((), ()))
MESH = pl.DeviceIdType.MESH


def kernel(
    mask_ref, hist_ref, k_ref, v_ref, qd_ref, q_hbm, ck_hbm, cv_hbm,
    out_ref, sout_ref,
    qv, qt, vown, km, vm, k0, v0, acc, m_ref, s0, s1, x0, x1,
    ck, cv, d0, d1, e0, e1, tops, totals, part, pair, got,
    local_sem, ss, rs, pss, prs,
):
    c = lax.axis_index("context")
    z = lax.rem(c, RING)
    half = c - z
    other = RING - half
    shard = ck_hbm.shape[1]

    q_copy = pltpu.make_async_copy(q_hbm, qv, local_sem.at[2, 0])
    q_copy.start()
    groups = STREAMS // GROUP

    def cache_copy(which, g):
        here, there = ((ck_hbm, ck), (cv_hbm, cv))[which]
        some = pl.ds(g * GROUP, GROUP)
        return pltpu.make_async_copy(here.at[some], there.at[some], local_sem.at[which, g])

    for g in range(groups):
        cache_copy(0, g).start()
        cache_copy(1, g).start()

    for ref in (vown, vm, v0):
        index = (Ellipsis, pl.ds(HEAD, VROWS - HEAD), slice(None))
        ref[index] = jnp.ones(ref.shape[:-2] + (VROWS - HEAD, ref.shape[-1]), BF16)

    barrier = pltpu.get_barrier_semaphore()
    for k in range(1, CTX):
        pl.semaphore_signal(
            barrier, inc=1, device_id={"context": lax.rem(c + k, CTX)}, device_id_type=MESH
        )
    vown[:HEAD, :] = v_ref[...].T

    own = (k_ref, vown.at[pl.ds(0, HEAD)])

    def main(what, slot):
        return (km.at[slot - 1], vm.at[slot - 1, pl.ds(0, HEAD)])[what], 2 * (slot - 1) + what

    def zero(what):
        return (k0, v0.at[pl.ds(0, HEAD)])[what], 6 + what

    def copy(source, target, to, sem):
        return pltpu.make_async_remote_copy(
            src_ref=source,
            dst_ref=target[0],
            send_sem=ss.at[sem],
            recv_sem=rs.at[target[1]],
            device_id={"context": to},
            device_id_type=MESH,
        )

    def arrived(target):
        copy(target[0], target, c, 0).wait_recv()

    sent = []

    def start(when, copies):
        @pl.when(when)
        def _():
            for one in copies:
                copy(*one).start()

        sent.append((when, copies))

    def both(make):
        return [make(what) for what in range(2)]

    def await_when(when, targets):
        @pl.when(when)
        def _():
            for target in targets:
                arrived(target)

    nxt = jnp.minimum(c + 1, CTX - 1)

    def pass_on(when, slot, w):
        await_when(c >= slot, [main(w, slot)])
        start(when, [(main(w, slot)[0], main(w, slot + 1), nxt, 2 * slot + w)])

    def first_to(when, what, targets):
        await_when(when, [zero(what)])
        start(when, [(zero(what)[0], zero(what), to, sem) for to, sem in targets])

    def first_both(when, to):
        for w in range(2):
            first_to(when, w, [(to, 6 + w)])

    def across(slot, to, w):
        start(c == slot, [(main(w, slot)[0], zero(w), to, 6 + w)])

    def stage_two():
        pass_on((c >= 1) & (c <= 14), 1, 1)
        across(1, 9, 0)
        across(1, 9, 1)
        first_to(c == 6, 0, [(4, 6)])

    def stage_three():
        first_to(c == 6, 1, [(4, 7)])
        start(c == 6, both(lambda w: (zero(w)[0], zero(w), 5, 8 + w)))
        start(c == 6, both(lambda w: (zero(w)[0], zero(w), 14, 10 + w)))

    def stage_one():
        pass_on((c >= 1) & (c <= 14), 1, 0)

    def stage_four():
        first_both(c == 7, 15)
        first_both(c == 4, 12)
        for w in range(2):
            await_when(c == 3, [main(w, 3)])
            across(3, 11, w)

    def stage_five():
        first_both(c == 5, 13)

    sb, xb = (s0, s1), (x0, x1)

    def turn_head(h):
        head = qv[:, h * HEAD : (h + 1) * HEAD].astype(F32) * SCALE
        qt[h] = head.astype(BF16).T

    def scores(keys, h, diagonal):
        s = jnp.dot(keys[...], qt[h], preferred_element_type=F32)
        if diagonal:
            key = lax.broadcasted_iota(jnp.int32, s.shape, 0)
            query = lax.broadcasted_iota(jnp.int32, s.shape, 1)
            s = jnp.where(key <= query, s, NEG)
        sb[h % 2][...] = s
        xb[h % 2][...] = jnp.max(s, axis=0, keepdims=True)

    def weigh(values, bias, h):
        top = xb[h % 2][...]
        if bias is None:
            new = shift = top
        else:
            old = m_ref[h, :1, :]
            new = jnp.maximum(old, top + bias)
            shift = new - bias
        p = jnp.exp2(sb[h % 2][...] - shift).astype(BF16)
        pv = jnp.dot(values[...], p, preferred_element_type=F32)
        if bias is None:
            acc[h] = pv
        else:
            acc[h] = acc[h] * jnp.exp2(old - new) + pv
        m_ref[h, :1, :] = new

    def finish(h):
        o = acc[h, :HEAD, :] / acc[h, HEAD : HEAD + 1, :]
        out_ref[:, h * HEAD : (h + 1) * HEAD] = o.astype(BF16).T

    def attend(keys, values, bias, diagonal=False, last=False):
        if diagonal:
            turn_head(0)
        scores(keys, 0, diagonal)
        for h in range(HEADS):
            if h + 1 < HEADS:
                if diagonal:
                    turn_head(h + 1)
                scores(keys, h + 1, diagonal)
            weigh(values, bias, h)
            if last and h:
                finish(h - 1)
        if last:
            finish(HEADS - 1)

    def attend_main(slot, when, last=False):
        allowed = mask_ref[c, jnp.maximum(c - slot, 0)] > 0
        bias = jnp.where(allowed, 0.0, NEG)

        @pl.when(when)
        def _():
            attend(km.at[slot - 1], vm.at[slot - 1], bias, last=last)

    def attend_zero(when, last=False):
        bias = jnp.where(mask_ref[c, 0] > 0, 0.0, NEG)

        @pl.when(when)
        def _():
            attend(k0, v0, bias, last=last)

    db, eb = (d0, d1), (e0, e1)
    col = lax.broadcasted_iota(jnp.int32, (ROWS, shard), 1)
    token = lax.rem(lax.broadcasted_iota(jnp.int32, (ROWS, shard), 0), TOKENS)
    ahead = col - token
    eye = lax.broadcasted_iota(jnp.int32, (ROWS, HEAD), 0) == lax.broadcasted_iota(
        jnp.int32, (ROWS, HEAD), 1
    )
    line = lax.broadcasted_iota(jnp.int32, (PACK - ROWS, HEAD), 0)

    def stream_scores(s, b):
        rows = qd_ref[s].astype(F32) * SCALE
        rows = jnp.concatenate(
            [rows[:, g * HEAD : (g + 1) * HEAD] for g in range(HEADS)], axis=0
        ).astype(BF16)
        x = lax.dot_general(rows, ck[s], NT, preferred_element_type=F32)
        limit = hist_ref[s] + 1 - c * shard
        x = jnp.where(ahead < limit, x, NEG)
        db[b][...] = x
        eb[b][...] = jnp.broadcast_to(jnp.max(x, axis=1, keepdims=True), (ROWS, HEAD))

    def stream_weigh(s, b):
        top = eb[b][:, :1]
        p = jnp.exp2(db[b][...] - top)
        total = jnp.sum(p, axis=1, keepdims=True)
        o = jnp.dot(p.astype(BF16), cv[s], preferred_element_type=F32) / total
        part[s, :ROWS, :] = o.astype(BF16)
        tops[s] = eb[b][...]
        totals[s] = jnp.broadcast_to(total, (ROWS, HEAD))

    def store_level(ref, s, level):
        level = jnp.sum(jnp.where(eye, level, 0.0), axis=0, keepdims=True)
        high = level.astype(BF16).astype(F32)
        mid = (level - high).astype(BF16).astype(F32)
        low = level - high - mid
        packed = jnp.where(line == 0, high, jnp.where(line == 1, mid, jnp.where(line == 2, low, 0.0)))
        ref[s, ROWS:, :] = packed.astype(BF16)

    def level_of(ref, s):
        rows = ref[s, ROWS:, :].astype(F32)
        row = rows[0:1, :] + rows[1:2, :] + rows[2:3, :]
        return jnp.sum(jnp.where(eye, row, 0.0), axis=1, keepdims=True)

    def streams(first, groups_now):
        stream_scores(first, 0)

        def group(i, carry):
            for u in range(GROUP):
                s = first + i * GROUP + u
                if u + 1 < GROUP:
                    stream_scores(s + 1, (u + 1) % 2)
                else:
                    stream_scores(jnp.minimum(s + 1, STREAMS - 1), (u + 1) % 2)
                stream_weigh(s, u % 2)
            return carry

        lax.fori_loop(0, groups_now, group, 0)

    def cross_copy():
        return pltpu.make_async_remote_copy(
            src_ref=part.at[pl.ds(other, RING)],
            dst_ref=pair,
            send_sem=pss.at[0],
            recv_sem=prs.at[0],
            device_id={"context": lax.rem(c + RING, CTX)},
            device_id_type=MESH,
        )

    def merge_pairs():
        cross_copy().wait()
        for n in range(RING):
            s = half + n
            one, two = level_of(part, s), level_of(pair, n)
            top = jnp.maximum(one, two)
            w_one, w_two = jnp.exp2(one - top), jnp.exp2(two - top)
            total = w_one + w_two
            value = part[s, :ROWS, :].astype(F32) * w_one + pair[n, :ROWS, :].astype(F32) * w_two
            part[s, :ROWS, :] = (value / total).astype(BF16)
            store_level(part, s, top + jnp.log(total) * LOG2E)

    def share():
        merge_pairs()
        for k in range(1, RING):
            ring_copy(k).start()
        got[z] = part[c]

    def ring_copy(k):
        to = half + lax.rem(z + k, RING)
        return pltpu.make_async_remote_copy(
            src_ref=part.at[to],
            dst_ref=got.at[z],
            send_sem=pss.at[k],
            recv_sem=prs.at[k],
            device_id={"context": to},
            device_id_type=MESH,
        )

    def diagonal():
        q_copy.wait()
        attend(k_ref, vown, None, True)

    def decode(first):
        if first == 0:
            for g in range(groups):
                cache_copy(0, g).wait()
                cache_copy(1, g).wait()
        streams(first, groups // 2)

    def levels_of_all():
        for s in range(STREAMS):
            store_level(part, s, tops[s] + jnp.log(totals[s]) * LOG2E)

    early = z <= 3
    ahead_of_all = early | (c < RING)

    @pl.when(ahead_of_all)
    def _():
        diagonal()

    @pl.when(early)
    def _():
        decode(0)
        decode(STREAMS // 2)
        levels_of_all()

    pl.semaphore_wait(barrier, CTX - 1)

    for w in range(2):
        start(c <= 14, [(own[w], main(w, 1), nxt, w)])
        start(c == 0, [(own[w], zero(w), 6, 6 + w)])
    start(c == 0, both(lambda w: (own[w], zero(w), 7, 8 + w)))

    @pl.when(early)
    def _():
        cross_copy().start()

    @pl.when(jnp.logical_not(ahead_of_all))
    def _():
        diagonal()

    stage_one()

    @pl.when(jnp.logical_not(early))
    def _():
        decode(0)

    stage_two()

    @pl.when(jnp.logical_not(early))
    def _():
        decode(STREAMS // 2)

    stage_three()

    @pl.when(jnp.logical_not(early))
    def _():
        levels_of_all()
        cross_copy().start()

    pass_on((c >= 2) & (c <= 14), 2, 0)
    across(2, 10, 0)
    first_to(c == 9, 0, [(8, 6)])
    attend_main(1, c >= 1)
    first_to(c == 9, 1, [(8, 7)])
    pass_on((c >= 2) & (c <= 14), 2, 1)
    across(2, 10, 1)
    @pl.when(c != 8)
    def _():
        share()

    stage_four()
    attend_main(2, c >= 2)
    stage_five()

    sooner = (c == 4) | (c == 6) | (c == 7) | (c == 9) | (c == 14)
    later = (c >= 4) & jnp.logical_not(sooner)
    await_when(c == 14, both(zero))
    attend_zero(sooner)
    await_when(c >= 4, both(lambda w: main(w, 3)))
    attend_main(3, sooner | (c == 3), True)
    attend_main(3, later)

    @pl.when(c == 8)
    def _():
        share()

    await_when(later & (c != 5), both(zero))
    attend_zero(later, True)

    @pl.when(c < 3)
    def _():
        for h in range(HEADS):
            finish(h)

    for k in range(1, RING):
        ring_copy(k).wait()
    levels = [level_of(got, n) for n in range(RING)]
    top = levels[0]
    for level in levels[1:]:
        top = jnp.maximum(top, level)
    total = jnp.zeros((ROWS, 1), F32)
    value = jnp.zeros((ROWS, HEAD), F32)
    for n, level in enumerate(levels):
        w = jnp.exp2(level - top)
        total += w
        value += got[n, :ROWS, :].astype(F32) * w
    value = value / total
    for g in range(HEADS):
        sout_ref[0, :, g * HEAD : (g + 1) * HEAD] = value[g * TOKENS : (g + 1) * TOKENS, :].astype(BF16)

    for when, some in sent:

        @pl.when(when)
        def _(some=some):
            for one in some:
                copy(*one).wait_send()


def local(turn_q, keys, values, block_mask, query_dec, cache_keys, cache_values, lengths):
    vmem = pl.BlockSpec(memory_space=pltpu.VMEM)
    smem = pl.BlockSpec(memory_space=pltpu.SMEM)
    anywhere = pl.BlockSpec(memory_space=pl.ANY)
    streams, shard, _ = cache_keys.shape
    return pl.pallas_call(
        kernel,
        out_shape=(
            jax.ShapeDtypeStruct(turn_q.shape, BF16),
            jax.ShapeDtypeStruct((1, TOKENS, HEADS * HEAD), BF16),
        ),
        in_specs=[smem, smem, vmem, vmem, vmem, anywhere, anywhere, anywhere],
        out_specs=(vmem, vmem),
        scratch_shapes=[
            pltpu.VMEM((BLOCK, HEADS * HEAD), BF16),
            pltpu.VMEM((HEADS, HEAD, BLOCK), BF16),
            pltpu.VMEM((VROWS, BLOCK), BF16),
            pltpu.VMEM((3, BLOCK, HEAD), BF16),
            pltpu.VMEM((3, VROWS, BLOCK), BF16),
            pltpu.VMEM((BLOCK, HEAD), BF16),
            pltpu.VMEM((VROWS, BLOCK), BF16),
            pltpu.VMEM((HEADS, VROWS, BLOCK), F32),
            pltpu.VMEM((HEADS, 8, BLOCK), F32),
            pltpu.VMEM((BLOCK, BLOCK), F32),
            pltpu.VMEM((BLOCK, BLOCK), F32),
            pltpu.VMEM((1, BLOCK), F32),
            pltpu.VMEM((1, BLOCK), F32),
            pltpu.VMEM((streams, shard, HEAD), BF16),
            pltpu.VMEM((streams, shard, HEAD), BF16),
            pltpu.VMEM((ROWS, shard), F32),
            pltpu.VMEM((ROWS, shard), F32),
            pltpu.VMEM((ROWS, HEAD), F32),
            pltpu.VMEM((ROWS, HEAD), F32),
            pltpu.VMEM((streams, ROWS, HEAD), F32),
            pltpu.VMEM((streams, ROWS, HEAD), F32),
            pltpu.VMEM((streams, PACK, HEAD), BF16),
            pltpu.VMEM((RING, PACK, HEAD), BF16),
            pltpu.VMEM((RING, PACK, HEAD), BF16),
            pltpu.SemaphoreType.DMA((3, STREAMS // GROUP)),
            pltpu.SemaphoreType.DMA((12,)),
            pltpu.SemaphoreType.DMA((8,)),
            pltpu.SemaphoreType.DMA((RING,)),
            pltpu.SemaphoreType.DMA((RING,)),
        ],
        compiler_params=pltpu.CompilerParams(
            collective_id=0, has_side_effects=True, vmem_limit_bytes=56 * 2**20
        ),
        cost_estimate=pl.CostEstimate(
            flops=6 * 10**9, bytes_accessed=11 * 2**20, transcendentals=11 * 10**6
        ),
    )(block_mask, lengths, keys, values, query_dec, turn_q, cache_keys, cache_values)


def solution(mesh):
    in_specs = (
        P(("dp", "context"), "tensor"),
        P(("dp", "context"), "tensor"),
        P(("dp", "context"), "tensor"),
        P(),
        P("dp", None, "tensor"),
        P("dp", "context", "tensor"),
        P("dp", "context", "tensor"),
        P("dp"),
    )
    out_specs = (P(("dp", "context"), "tensor"), P(("dp", "context"), None, "tensor"))
    return jax.shard_map(local, mesh=mesh, in_specs=in_specs, out_specs=out_specs, check_vma=False)
```
